32 devices in a mesh: groups: 2 (over x), blk: 16 (over z, y, core).
Axes of the slice: x: 2, y: 2, z: 4, core: 2. Of those that a mesh axis runs over, the one named last changes fastest.
Arguments:
- train_acts: bfloat16 [4096, 768], P(('groups', 'blk')), parts along dimension 0, may hold values from -6 to 6
- train_grads: bfloat16 [4096, 2048], P(('groups', 'blk')), parts along dimension 0, may hold values from -0.059814453 to 0.059814453
- train_expert: int32 [4096, 1], P(('groups', 'blk')), parts along dimension 0, may hold values from 0 to 1; in each aligned block of 128 rows (0 to 127, 128 to 255, ...) at most 96 rows name the same one
- train_doc: int32 [4096], P(('groups', 'blk')), parts along dimension 0, may hold values from 0 to 3
- query_acts: bfloat16 [64, 768], P('blk'), may hold values from -6 to 6
- query_grads: bfloat16 [64, 2048], P('blk'), may hold values from -0.059814453 to 0.059814453
- query_expert: int32 [64, 1], P('blk'), may hold values from 0 to 1; in each aligned block of 4 rows (0 to 3, 4 to 7, ...) at most 3 rows name the same one
- query_ids: int32 [64], P('blk'), may hold values from 0 to 1
- basis_out: bfloat16 [2, 2048, 2048], P(None, None, 'blk'), may hold values from -0.125 to 0.125
- basis_in: bfloat16 [2, 768, 768], P(None, None, 'blk'), may hold values from -0.21875 to 0.21875
- eigenvalues: bfloat16 [2, 2048, 768], P(None, 'blk'), may hold values from 0.019897461 to 5
Outputs:
- scores: float32 [128, 32], P(('groups', 'blk')), parts along dimension 0
The draws below stay inside these ranges and needn't reach their ends.
There are 2 independent parts, one for each index of `groups`. The reference program is written for one: setup_inputs(seed, part) draws one part's arguments, and reference() takes and returns one part's arrays. A program takes and returns all parts, laid end to end along the dimension named above; an argument that names none is the same for every part. Nothing has to cross between parts.
Inputs may be any that keep to these rules, and one draw needn't show every extreme that they name: `train_expert`: the rows of one device name each expert at most 96 times; in every draw some device's rows name one expert exactly 96 times. `query_expert`: the rows of one device name each expert at most 3 times; in every draw some device's rows name one expert exactly 3 times.
All inputs are finite; a program needn't handle non-finite values.
Results may differ from the reference program's by a relative error of at most 0.0053.
Values may be sent and summed in bfloat16 or wider, within the bound.
A program may use at most 128 MiB of HBM per device.

```python
import math
import jax
import jax.numpy as jnp
import numpy as np
from jax import lax

D = 2048
F = 768
EXPERTS = 2
T_DEV = 128
DOCS_DEV = 4
QTOK_DEV = 4
QRY_DEV = 2
CAP = 96
QCAP = 3
TRAIN = 2048
QTOK = 64
DOCS = 64
QUERIES = 32
N_BLK = 16


def touch_ends(values, key, low, top_value):
    shape = values.shape
    index_at = [jax.random.randint(jax.random.fold_in(key, axis), (), 0, shape[axis]) for axis in range(len(shape))]
    values = values.at[tuple(index_at)].set(low)
    longest = shape.index(max(shape))
    index_at[longest] = (index_at[longest] + 1) % shape[longest]
    return values.at[tuple(index_at)].set(top_value)


def shard_levels(key, extent, shards, low, high):
    level, own = 1.0, jax.random.fold_in(key, 6)
    for position, shards_of in shards:
        steps = jnp.exp(jax.random.uniform(jax.random.fold_in(own, position), (shards_of,), jnp.float32, low / len(shards), high / len(shards)))
        level = level * jnp.repeat(steps, extent[position] // shards_of).reshape([-1 if axis == position else 1 for axis in range(len(extent))])
    return level


def shared_out(own_key, own, number, rows, count, top, bound, skew):
    ranking = jax.random.permutation(own_key, count)
    heavy_load, usual = load_shares(count, rows * top, bound, skew, True), load_shares(count, rows * top, bound, skew, False)
    places = jnp.arange(count)

    def named(tallies, rotation):
        used = int((tallies > 0).sum())
        fixed = max(1, used // 4)
        passed = fixed + (places - fixed + rotation * (used - fixed)) % max(1, count - fixed)
        return jnp.zeros((count,), jnp.int32).at[ranking[jnp.where(places < fixed, places, passed)]].set(jnp.asarray(tallies, jnp.int32))

    tallies = jnp.where(number % 4 == 0, named(heavy_load, number // 4), named(usual, number - number // 4 - 1))
    mixed = jax.random.permutation(jax.random.fold_in(own, 3), count)
    source_of, receiver = mixed[0:count // 2 * 2:2], mixed[1:count // 2 * 2:2]
    slack = jnp.minimum(tallies[source_of] - 1, bound - tallies[receiver]) // 2
    slack = jnp.where((source_of == ranking[0]) | (receiver == ranking[0]) | (tallies[receiver] == 0), 0, jnp.maximum(slack, 0))
    passed = jax.random.randint(jax.random.fold_in(own, 4), (count // 2,), 0, 1 << 20) % (slack + 1)
    tallies = tallies.at[source_of].add(-passed).at[receiver].add(passed)
    members = jnp.searchsorted(jnp.cumsum(tallies), jnp.arange(rows * top), side="right").astype(jnp.int32)
    grid = members.reshape(top, rows).T
    grid = grid[jax.random.permutation(jax.random.fold_in(own, 1), rows)]
    rotation = jax.random.randint(jax.random.fold_in(own, 2), (rows, 1), 0, top)
    return jnp.take_along_axis(grid, (jnp.arange(top)[None, :] + rotation) % top, axis=1)


def load_shares(count, total, most, skew, full):
    loads = [(1 << 20) // math.isqrt(standing ** skew) + 1 for standing in range(1, count + 1)]
    largest = most if full else min(most, max(-(-total // count), total * loads[0] // sum(loads)))
    least = 1 if total - largest >= count - 1 else 0
    given, surplus = [largest] + [least] * (count - 1), total - largest - least * (count - 1)
    while surplus > 0:
        movable = [i for i in range(1, count) if given[i] < largest] or [i for i in range(1, count) if given[i] < most]
        whole, left = sum([loads[i] for i in movable]), surplus
        for i in movable:
            addition = min(most - given[i], max(1, left * loads[i] // whole), surplus)
            given[i] = given[i] + addition
            surplus = surplus - addition
    return np.array(given)


def bell_draw(own_key, shape, deviation, limit, cuts=(), held_as=jnp.bfloat16):
    values = deviation * jax.random.normal(own_key, shape, jnp.float32)
    if cuts:
        values = values * shard_levels(own_key, shape, cuts, -0.22, 0.18)
    return jnp.clip(values, -limit, limit).astype(held_as)


def setup_inputs(seed: int = 0, part: int = 0) -> dict:
    key_of = jax.random.split(jax.random.key(seed), 12)
    part_keys = jax.random.split(jax.random.fold_in(key_of[11], part), 12)
    train_acts = bell_draw(part_keys[0], (TRAIN, F), 1.0, 6.0, ((0, 16),))
    train_grads = bell_draw(part_keys[1], (TRAIN, D), 0.01, 0.059814453, ((0, 16),))
    train_expert_keys = jax.random.split(jax.random.fold_in(part_keys[2], 1), TRAIN // T_DEV)
    train_expert_turns = jax.random.permutation(jax.random.fold_in(part_keys[2], 3), TRAIN // T_DEV)
    train_expert = jax.vmap(lambda own, number: shared_out(jax.random.fold_in(part_keys[2], 2), own, number, T_DEV, EXPERTS, 1, CAP, 2))(train_expert_keys, train_expert_turns).reshape((TRAIN, 1))
    train_doc = touch_ends(jax.random.randint(part_keys[3], (TRAIN,), 0, DOCS_DEV), jax.random.fold_in(part_keys[3], 1), 0, DOCS_DEV - 1).astype(jnp.int32)
    query_acts = bell_draw(key_of[4], (QTOK, F), 1.0, 6.0, ((0, 16),))
    query_grads = bell_draw(key_of[5], (QTOK, D), 0.01, 0.059814453, ((0, 16),))
    query_expert_keys = jax.random.split(jax.random.fold_in(key_of[6], 1), QTOK // QTOK_DEV)
    query_expert_turns = jax.random.permutation(jax.random.fold_in(key_of[6], 3), QTOK // QTOK_DEV)
    query_expert = jax.vmap(lambda own, number: shared_out(jax.random.fold_in(key_of[6], 2), own, number, QTOK_DEV, EXPERTS, 1, QCAP, 2))(query_expert_keys, query_expert_turns).reshape((QTOK, 1))
    query_ids = touch_ends(jax.random.randint(key_of[7], (QTOK,), 0, QRY_DEV), jax.random.fold_in(key_of[7], 1), 0, QRY_DEV - 1).astype(jnp.int32)
    basis_out = bell_draw(key_of[8], (EXPERTS, D, D), D ** -0.5, 0.125, ((2, 16),))
    basis_in = bell_draw(key_of[9], (EXPERTS, F, F), F ** -0.5, 0.21875, ((2, 16),))
    eigenvalues = jnp.clip(jnp.exp(math.log(5.0) - 5.526601 * jax.random.uniform(key_of[10], (EXPERTS, D, F), jnp.float32) ** shard_levels(key_of[10], (EXPERTS, D, F), ((1, 16),), -0.2, 0.2)), 0.019897461, 5.0).astype(jnp.bfloat16)
    return {"train_acts": train_acts, "train_grads": train_grads, "train_expert": train_expert, "train_doc": train_doc, "query_acts": query_acts, "query_grads": query_grads, "query_expert": query_expert, "query_ids": query_ids, "basis_out": basis_out, "basis_in": basis_in, "eigenvalues": eigenvalues}


DAMPING = 0.05


def rotate(rows, experts, basis):
    result = jnp.zeros((rows.shape[0], basis.shape[2]), jnp.float32)
    for which in range(EXPERTS):
        turned = jnp.dot(rows, basis[which], preferred_element_type=jnp.float32)
        result = jnp.where((experts == which)[:, None], turned, result)
    return result.astype(jnp.bfloat16)


def reference(train_acts, train_grads, train_expert, train_doc, query_acts, query_grads, query_expert, query_ids, basis_out, basis_in, eigenvalues):
    train_exp = train_expert[:, 0]
    query_exp = query_expert[:, 0]
    train_rot_grad = rotate(train_grads, train_exp, basis_out)
    train_rot_act = rotate(train_acts, train_exp, basis_in)
    query_rot_grad = rotate(query_grads, query_exp, basis_out)
    query_rot_act = rotate(query_acts, query_exp, basis_in)
    owner = jnp.arange(QTOK, dtype=jnp.int32) // QTOK_DEV
    global_ids = owner * QRY_DEV + query_ids
    columns = jnp.arange(QUERIES, dtype=jnp.int32)
    picked = []
    for which in range(EXPERTS):
        order = jnp.argsort((query_exp != which).astype(jnp.int32), stable=True)[: QCAP * N_BLK]
        valid = query_exp[order] == which
        grads_e = jnp.where(valid[:, None], query_rot_grad[order].astype(jnp.float32), 0.0)
        acts_e = query_rot_act[order].astype(jnp.float32)
        ids_e = jnp.where(valid, global_ids[order], -1)
        table_e = (ids_e[:, None] == columns[None, :]).astype(jnp.float32)
        picked.append((grads_e, acts_e, table_e))
    scale = eigenvalues.astype(jnp.float32) + DAMPING

    def block(index):
        start = index * T_DEV
        grads = lax.dynamic_slice_in_dim(train_rot_grad, start, T_DEV, 0)
        acts = lax.dynamic_slice_in_dim(train_rot_act, start, T_DEV, 0)
        exps = lax.dynamic_slice_in_dim(train_exp, start, T_DEV, 0)
        docs = lax.dynamic_slice_in_dim(train_doc, start, T_DEV, 0)
        total = jnp.zeros((DOCS_DEV, QUERIES), jnp.float32)
        for which in range(EXPERTS):
            mats = []
            for doc in range(DOCS_DEV):
                keep = ((docs == doc) & (exps == which)).astype(jnp.bfloat16)
                summed = jnp.dot((grads * keep[:, None]).T, acts, preferred_element_type=jnp.float32)
                mats.append((summed / scale[which]).astype(jnp.bfloat16))
            stacked = jnp.stack(mats).astype(jnp.float32)
            grads_e, acts_e, table_e = picked[which]
            image = jnp.einsum("sf,kdf->ksd", acts_e, stacked)
            token = jnp.einsum("ksd,sd->ks", image, grads_e)
            total = total + jnp.dot(token, table_e, precision=lax.Precision.HIGHEST)
        return total

    blocks = lax.map(block, jnp.arange(N_BLK, dtype=jnp.int32))
    return blocks.reshape(DOCS, QUERIES)
```

```python
import jax
import jax.numpy as jnp
from jax import lax
from jax.experimental import pallas as pl
from jax.experimental.pallas import tpu as pltpu
from jax.sharding import PartitionSpec as P

DOCS_DEV = 4
QRY_DEV = 2
CAP = 96
QCAP = 3
DAMPING = 0.05
LANES = 128
COPIES = 25
LOCALS = 5
MESH = pl.DeviceIdType.MESH


def kernel(
    grads_in, acts_in, bo_in, ei_in, pk_in, out_ref,
    rows, acts, bo, ei, biq, bit, rot_a, qn, qat, qgt, rc, gt, tok, got,
    send, recv, local,
):
    x = lax.axis_index("groups")
    b = lax.axis_index("blk")
    c, y, z = b % 2, (b // 2) % 2, b // 4
    z1 = z + 1 - 2 * (z % 2)
    z2 = (z + 2) % 4

    def at(xx, zz, yy, cc):
        return (xx, (zz * 2 + yy) * 2 + cc)

    to_z1, to_z2 = at(x, z1, y, c), at(x, z2, y, c)
    to_y, to_x = at(x, z, 1 - y, c), at(1 - x, z, y, c)
    to_c, to_d = at(x, z, y, 1 - c), at(x, z1, 1 - y, c)
    barrier = pltpu.get_barrier_semaphore()
    for peer in (to_z1, to_z2, to_y, to_x, to_c, to_d):
        pl.semaphore_signal(barrier, inc=1, device_id=peer, device_id_type=MESH)

    def put(i, src, dst, peer):
        return pltpu.make_async_remote_copy(
            src_ref=src, dst_ref=dst, send_sem=send.at[i], recv_sem=recv.at[i],
            device_id=peer, device_id_type=MESH,
        )

    T = LANES
    ox = 1 - x
    cp = [
        put(0, grads_in, rows.at[pl.ds(T, T)], to_z1),
        put(1, acts_in, acts.at[pl.ds(T, T)], to_z1),
        put(2, grads_in, rows.at[pl.ds(2 * T, T)], to_y),
        put(3, acts_in, acts.at[pl.ds(2 * T, T)], to_y),
        put(4, rows.at[pl.ds(T, T)], rows.at[pl.ds(3 * T, T)], to_y),
        put(5, acts.at[pl.ds(T, T)], acts.at[pl.ds(3 * T, T)], to_y),
        put(6, bo_in.at[x], bo.at[1, x], to_z2),
        put(7, ei_in.at[x], ei.at[1, x], to_z2),
        put(8, bo.at[1, x], bo.at[1, x], to_x),
        put(9, ei.at[1, x], ei.at[1, x], to_x),
        put(10, bo_in, bo.at[2], to_c),
        put(11, ei_in, ei.at[2], to_c),
        put(12, bo.at[1, x], bo.at[3, x], to_c),
        put(13, ei.at[1, x], ei.at[3, x], to_c),
        put(14, bo.at[1, ox], bo.at[3, ox], to_c),
        put(15, ei.at[1, ox], ei.at[3, ox], to_c),
        put(16, pk_in.at[x], biq.at[x, 1], to_z2),
        put(17, biq.at[x, pl.ds(0, 2)], biq.at[x, pl.ds(2, 2)], to_z1),
        put(18, biq.at[x, pl.ds(0, 4)], biq.at[x, pl.ds(4, 4)], to_y),
        put(19, biq.at[x, pl.ds(0, 8)], biq.at[x, pl.ds(0, 8)], to_x),
        put(20, biq.at[x, pl.ds(0, 8)], biq.at[x, pl.ds(8, 8)], to_c),
        put(21, biq.at[ox, pl.ds(0, 8)], biq.at[ox, pl.ds(8, 8)], to_c),
        put(22, tok.at[1], got.at[0], to_z1),
        put(23, tok.at[2], got.at[1], to_y),
        put(24, tok.at[3], got.at[2], to_d),
    ]
    here = [
        pltpu.make_async_copy(pk_in.at[x], biq.at[x, 0], local.at[0]),
        pltpu.make_async_copy(grads_in, rows.at[pl.ds(0, T)], local.at[1]),
        pltpu.make_async_copy(acts_in, acts.at[pl.ds(0, T)], local.at[2]),
        pltpu.make_async_copy(bo_in, bo.at[0], local.at[3]),
        pltpu.make_async_copy(ei_in, ei.at[0], local.at[4]),
    ]
    for one in here:
        one.start()
    pl.semaphore_wait(barrier, 6)

    def go(*which):
        for i in which:
            cp[i].start()

    def came(*which):
        for i in which:
            cp[i].wait_recv()

    go(16, 1, 0, 6, 7, 3, 2, 11, 10)
    here[0].wait()
    came(16)
    go(17)
    came(17)
    go(18)
    came(1, 0)
    go(5, 4)
    came(18)
    go(20, 19)
    for one in here[1:]:
        one.wait()

    def recips(j):
        for e in range(2):
            def step(i, _):
                at_rows = pl.ds(pl.multiple_of(i * 16, 16), 16)
                rc[e, j, at_rows, :] = 1.0 / (ei[j, e, at_rows, :].astype(jnp.float32) + DAMPING)
                return 0
            lax.fori_loop(0, 8, step, 0)

    recips(0)
    came(11, 10)
    recips(2)
    came(6, 7)
    go(9, 8, 13, 12)
    came(19)
    go(21)
    came(20, 21)

    for other in range(16):
        oc, oy, oz = other % 2, (other // 2) % 2, other // 4
        slot = (
            jnp.where(z // 2 != oz // 2, 1, 0)
            + jnp.where(z % 2 != oz % 2, 2, 0)
            + jnp.where(y != oy, 4, 0)
            + jnp.where(c != oc, 8, 0)
        )
        for e in range(2):
            bit[e, 48 * other : 48 * other + 48, :] = biq[e, slot, 0:48, :]
        qn[16 * other : 16 * other + 16, :] = biq[0, slot, 48:64, :]

    s_at = lax.broadcasted_iota(jnp.int32, (T, 2 * T), 0)
    r_at = lax.broadcasted_iota(jnp.int32, (T, 2 * T), 1)
    quarter = []
    for j in range(4):
        pick = jnp.where(r_at == 4 * s_at + j, 1.0, 0.0).astype(jnp.bfloat16)
        quarter.append(
            jnp.dot(pick, qn[...], preferred_element_type=jnp.float32).astype(jnp.bfloat16)
        )
    Q = 4 * T
    rows[Q : Q + T, 0:768] = quarter[0]
    rows[Q : Q + T, 768:1536] = quarter[1]
    rows[Q : Q + T, 1536:2048] = quarter[2][:, 0:512]
    acts[Q : Q + T, 0:256] = quarter[2][:, 512:768]
    acts[Q : Q + T, 256:896] = quarter[3][:, 0:640]
    ident = quarter[3][:, 640:768].astype(jnp.float32)

    def code_of(slot):
        at_rows = pl.ds(pl.multiple_of(slot * T, T), T)
        return at_rows, acts[at_rows, 768:896].astype(jnp.float32)

    came(3, 2, 5, 4)

    def turn_acts(slot, _):
        at_rows, code = code_of(slot)
        second = jnp.concatenate([code] * 6, axis=1) >= 4.0
        each = [
            lax.dot_general(
                acts[at_rows, 0:768], bit[e], (((1,), (1,)), ((), ())),
                preferred_element_type=jnp.float32,
            )
            for e in range(2)
        ]
        rot_a[at_rows, :] = jnp.where(second, each[1], each[0]).astype(jnp.bfloat16)
        return 0

    lax.fori_loop(0, 5, turn_acts, 0)
    _, qcode = code_of(4)
    qsecond = jnp.concatenate([qcode] * 6, axis=1) >= 4.0
    turned = rot_a[Q : Q + T, :].astype(jnp.float32)
    qat[0] = jnp.where(qsecond, 0.0, turned).T.astype(jnp.bfloat16)
    qat[1] = jnp.where(qsecond, turned, 0.0).T.astype(jnp.bfloat16)
    tok[...] = jnp.zeros_like(tok)

    def columns(first, last):
        def turn_grads(slot, _):
            at_rows, code = code_of(slot)
            second = jnp.concatenate([code] * 2, axis=1) >= 4.0
            each = [
                jnp.dot(
                    rows[at_rows, :],
                    jnp.concatenate([bo[first, e], bo[last, e]], axis=1),
                    preferred_element_type=jnp.float32,
                )
                for e in range(2)
            ]
            gt[slot] = jnp.where(second, each[1], each[0]).T.astype(jnp.bfloat16)
            return 0

        lax.fori_loop(0, 5, turn_grads, 0)
        qgt[...] = gt[4].astype(jnp.float32)

        def score(slot, _):
            at_rows, code = code_of(slot)
            wide = jnp.concatenate([code] * 6, axis=1)
            ra = rot_a[at_rows, :].astype(jnp.float32)
            for doc in range(DOCS_DEV):
                image = jnp.zeros((2 * T, T), jnp.float32)
                for e in range(2):
                    kept = jnp.where(wide == float(4 * e + doc), ra, 0.0).astype(jnp.bfloat16)
                    summed = jnp.dot(gt[slot], kept, preferred_element_type=jnp.float32)
                    scale = jnp.concatenate([rc[e, first], rc[e, last]], axis=0)
                    mat = (summed * scale).astype(jnp.bfloat16)
                    image = image + jnp.dot(mat, qat[e], preferred_element_type=jnp.float32)
                part = jnp.sum(image * qgt[...], axis=0, keepdims=True)
                tok[slot, doc : doc + 1, :] = tok[slot, doc : doc + 1, :] + part
            return 0

        lax.fori_loop(0, 4, score, 0)

    columns(0, 2)
    came(9, 8)
    go(15, 14)
    recips(1)
    came(13, 12, 15, 14)
    recips(3)
    columns(1, 3)

    go(22, 23, 24)
    s_f = lax.broadcasted_iota(jnp.int32, (T, T), 0)
    q_f = lax.broadcasted_iota(jnp.int32, (T, T), 1).astype(jnp.float32)
    owner = ((s_f // 4) * QRY_DEV).astype(jnp.float32)
    table = jnp.where(owner + ident == q_f, 1.0, 0.0)
    came(22, 23, 24)
    total = tok[0] + got[0] + got[1] + got[2]
    res = jnp.dot(
        total, table, precision=lax.Precision.HIGHEST, preferred_element_type=jnp.float32
    )
    out_ref[...] = res[0:4, 0:32]
    for one in cp:
        one.wait_send()


def fused(
    train_acts, train_grads, train_expert, train_doc, query_acts, query_grads,
    query_expert, query_ids, basis_out, basis_in, eigenvalues,
):
    bf = jnp.bfloat16
    code = (train_expert * 4 + train_doc[:, None]).astype(bf)
    acts_in = jnp.concatenate([train_acts, jnp.broadcast_to(code, (LANES, LANES))], axis=1)
    qcode = jnp.broadcast_to((query_expert * 4).astype(bf), (4, LANES))
    qident = jnp.broadcast_to(query_ids.astype(bf)[:, None], (4, LANES))
    qpack = jnp.concatenate([query_grads, query_acts, qcode, qident], axis=1).reshape(1, 16, 768)
    qpack = jnp.concatenate([qpack, jnp.zeros_like(qpack)], axis=0)
    pk_in = jnp.concatenate([jnp.swapaxes(basis_in, 1, 2), qpack], axis=1)
    anywhere = pl.BlockSpec(memory_space=pl.ANY)
    f32 = jnp.float32
    return pl.pallas_call(
        kernel,
        out_shape=jax.ShapeDtypeStruct((4, 32), f32),
        in_specs=[anywhere] * 5,
        out_specs=pl.BlockSpec(memory_space=pltpu.VMEM),
        scratch_shapes=[
            pltpu.VMEM((5 * LANES, 2048), bf),
            pltpu.VMEM((5 * LANES, 896), bf),
            pltpu.VMEM((4, 2, 2048, LANES), bf),
            pltpu.VMEM((4, 2, LANES, 768), bf),
            pltpu.VMEM((2, 16, 64, 768), bf),
            pltpu.VMEM((2, 768, 768), bf),
            pltpu.VMEM((5 * LANES, 768), bf),
            pltpu.VMEM((2 * LANES, 768), bf),
            pltpu.VMEM((2, 768, LANES), bf),
            pltpu.VMEM((2 * LANES, LANES), f32),
            pltpu.VMEM((2, 4, LANES, 768), f32),
            pltpu.VMEM((5, 2 * LANES, LANES), bf),
            pltpu.VMEM((4, 8, LANES), f32),
            pltpu.VMEM((3, 8, LANES), f32),
            pltpu.SemaphoreType.DMA((COPIES,)),
            pltpu.SemaphoreType.DMA((COPIES,)),
            pltpu.SemaphoreType.DMA((LOCALS,)),
        ],
        compiler_params=pltpu.CompilerParams(
            collective_id=0, has_side_effects=True, vmem_limit_bytes=48 * 2**20
        ),
    )(train_grads, acts_in, basis_out, eigenvalues, pk_in)


def slot_table(experts, capacity, count):
    rows = experts.shape[0]
    place = jnp.arange(rows, dtype=jnp.int32)
    ahead = (experts[:, None] == experts[None, :]) & (place[None, :] < place[:, None])
    rank = jnp.sum(ahead.astype(jnp.int32), axis=1)
    target = experts * capacity + rank
    source = (
        jnp.zeros((count * capacity,), jnp.int32).at[target].set(jnp.arange(rows, dtype=jnp.int32))
    )
    filled = jnp.zeros((count * capacity,), jnp.int32).at[target].set(1)
    return (source.reshape(count, capacity), filled.reshape(count, capacity))


def turner(rows, piece):
    return jnp.einsum("ecd,edn->ecn", rows, piece, preferred_element_type=jnp.float32)


def body(
    train_acts,
    train_grads,
    train_expert,
    train_doc,
    query_acts,
    query_grads,
    query_expert,
    query_ids,
    basis_out,
    basis_in,
    eigenvalues,
):
    count = basis_out.shape[0]
    train_src, train_fill = slot_table(train_expert[:, 0], CAP, count)
    query_src, query_fill = slot_table(query_expert[:, 0], QCAP, count)
    source = jnp.concatenate([train_src, query_src + train_acts.shape[0]], axis=1)
    filled = jnp.concatenate([train_fill, query_fill], axis=1)
    weight = filled.astype(jnp.bfloat16)[:, :, None]
    grads_in = jnp.concatenate([train_grads, query_grads], axis=0)[source] * weight
    acts_in = jnp.concatenate([train_acts, query_acts], axis=0)[source] * weight
    slot_doc = train_doc[train_src]
    queries_total = QRY_DEV * lax.axis_size("blk")
    global_ids = jnp.where(
        query_fill == 1, lax.axis_index("blk") * QRY_DEV + query_ids[query_src], -1
    )
    rot_grads = turner(grads_in, lax.all_gather(basis_out, "blk", axis=2, tiled=True))
    rot_acts = turner(acts_in, lax.all_gather(basis_in, "blk", axis=2, tiled=True))
    rot_grads = rot_grads.astype(jnp.bfloat16)
    rot_acts = rot_acts.astype(jnp.bfloat16)
    train_g = rot_grads[:, :CAP]
    train_a = rot_acts[:, :CAP]
    query_g = rot_grads[:, CAP:]
    query_a = rot_acts[:, CAP:]
    doc_masks = [
        ((slot_doc == doc) & (train_fill == 1)).astype(jnp.bfloat16) for doc in range(DOCS_DEV)
    ]
    scale = lax.all_gather(eigenvalues, "blk", axis=1, tiled=True).astype(jnp.float32) + DAMPING
    mats = []
    for mask in doc_masks:
        summed = jnp.einsum(
            "ecn,ecf->enf", train_g * mask[:, :, None], train_a, preferred_element_type=jnp.float32
        )
        mats.append((summed / scale).astype(jnp.bfloat16))
    doc_mats = jnp.stack(mats)
    piece_g, piece_a, piece_ids = lax.all_gather(
        (query_g, query_a, global_ids), "blk", axis=1, tiled=True
    )
    image = jnp.einsum("esf,kedf->kesd", piece_a, doc_mats, preferred_element_type=jnp.float32)
    token = jnp.einsum("kesd,esd->esk", image, piece_g.astype(jnp.float32))
    table = (
        piece_ids.reshape(-1)[:, None] == jnp.arange(queries_total, dtype=jnp.int32)[None, :]
    ).astype(jnp.float32)
    return jnp.dot(token.reshape(-1, DOCS_DEV).T, table, precision=lax.Precision.HIGHEST)


def solution(mesh):
    in_specs = (
        P(("groups", "blk"), None),
        P(("groups", "blk"), None),
        P(("groups", "blk"), None),
        P(("groups", "blk")),
        P("blk", None),
        P("blk", None),
        P("blk", None),
        P("blk"),
        P(None, None, "blk"),
        P(None, None, "blk"),
        P(None, "blk", None),
    )
    out_specs = P(("groups", "blk"), None)
    sizes = (mesh.shape["groups"], mesh.shape["blk"])
    chosen = fused if sizes == (2, 16) else body
    return jax.shard_map(chosen, mesh=mesh, in_specs=in_specs, out_specs=out_specs, check_vma=False)
```

```python
import jax
import jax.numpy as jnp
from jax import lax
from jax.experimental import pallas as pl
from jax.experimental.pallas import tpu as pltpu
from jax.sharding import PartitionSpec as P

DOCS_DEV = 4
QRY_DEV = 2
CAP = 96
QCAP = 3
DAMPING = 0.05
LANES = 128
COPIES = 40
PARTS = 4
LOCALS = 5
MESH = pl.DeviceIdType.MESH


def kernel(
    grads_in, acts_in, bo_in, ei_in, pk_in, out_ref,
    rows, acts, bo, ei, biq, bit, rot_a, qn, qat, qgt, rc, gt, tok, got,
    send, recv, local,
):
    x = lax.axis_index("groups")
    b = lax.axis_index("blk")
    c, y, z = b % 2, (b // 2) % 2, b // 4
    z1 = z + 1 - 2 * (z % 2)
    z2 = (z + 2) % 4

    def at(xx, zz, yy, cc):
        return (xx, (zz * 2 + yy) * 2 + cc)

    to_z1, to_z2 = at(x, z1, y, c), at(x, z2, y, c)
    to_y, to_x = at(x, z, 1 - y, c), at(1 - x, z, y, c)
    to_c, to_d = at(x, z, y, 1 - c), at(x, z1, 1 - y, c)
    used = []
    barrier = pltpu.get_barrier_semaphore()
    for peer in (to_z1, to_z2, to_y, to_x, to_c, to_d):
        pl.semaphore_signal(barrier, inc=1, device_id=peer, device_id_type=MESH)

    def put(i, src, dst, peer):
        return pltpu.make_async_remote_copy(
            src_ref=src, dst_ref=dst, send_sem=send.at[i], recv_sem=recv.at[i],
            device_id=peer, device_id_type=MESH,
        )

    T = LANES
    ox = 1 - x
    R, K = T // PARTS, 2048 // PARTS
    count = [0]

    def next_put(src, dst, peer):
        count[0] += 1
        return put(count[0] - 1, src, dst, peer)

    def row_parts(src, first, peer):
        return [
            next_put(src.at[pl.ds(R * k, R)], rows.at[pl.ds(first + R * k, R)], peer)
            for k in range(PARTS)
        ]

    rows_z = row_parts(grads_in, T, to_z1)
    rows_y = row_parts(grads_in, 2 * T, to_y)
    rows_d = row_parts(rows.at[pl.ds(T, T)], 3 * T, to_y)
    bo_z = [
        next_put(bo_in.at[x, pl.ds(K * k, K)], bo.at[1, x, pl.ds(K * k, K)], to_z2)
        for k in range(PARTS)
    ]
    bo_x = [
        next_put(bo.at[1, x, pl.ds(K * k, K)], bo.at[1, x, pl.ds(K * k, K)], to_x)
        for k in range(PARTS)
    ]
    acts_z = next_put(acts_in, acts.at[pl.ds(T, T)], to_z1)
    acts_y = next_put(acts_in, acts.at[pl.ds(2 * T, T)], to_y)
    acts_d = next_put(acts.at[pl.ds(T, T)], acts.at[pl.ds(3 * T, T)], to_y)
    ei_z = next_put(ei_in.at[x], ei.at[1, x], to_z2)
    ei_x = next_put(ei.at[1, x], ei.at[1, x], to_x)
    bo_c = next_put(bo_in, bo.at[2], to_c)
    ei_c = next_put(ei_in, ei.at[2], to_c)
    bo_c1 = next_put(bo.at[1, x], bo.at[3, x], to_c)
    ei_c1 = next_put(ei.at[1, x], ei.at[3, x], to_c)
    bo_c2 = next_put(bo.at[1, ox], bo.at[3, ox], to_c)
    ei_c2 = next_put(ei.at[1, ox], ei.at[3, ox], to_c)
    pk_z2 = next_put(pk_in.at[x], biq.at[x, 1], to_z2)
    pk_z1 = next_put(biq.at[x, pl.ds(0, 2)], biq.at[x, pl.ds(2, 2)], to_z1)
    pk_y = next_put(biq.at[x, pl.ds(0, 4)], biq.at[x, pl.ds(4, 4)], to_y)
    pk_x = next_put(biq.at[x, pl.ds(0, 8)], biq.at[x, pl.ds(0, 8)], to_x)
    pk_c1 = next_put(biq.at[x, pl.ds(0, 8)], biq.at[x, pl.ds(8, 8)], to_c)
    pk_c2 = next_put(biq.at[ox, pl.ds(0, 8)], biq.at[ox, pl.ds(8, 8)], to_c)
    tok_z = next_put(tok.at[1], got.at[0], to_z1)
    tok_y = next_put(tok.at[2], got.at[1], to_y)
    tok_d = next_put(tok.at[3], got.at[2], to_d)
    here = [
        pltpu.make_async_copy(pk_in.at[x], biq.at[x, 0], local.at[0]),
        pltpu.make_async_copy(grads_in, rows.at[pl.ds(0, T)], local.at[1]),
        pltpu.make_async_copy(acts_in, acts.at[pl.ds(0, T)], local.at[2]),
        pltpu.make_async_copy(bo_in, bo.at[0], local.at[3]),
        pltpu.make_async_copy(ei_in, ei.at[0], local.at[4]),
    ]
    for one in here:
        one.start()
    pl.semaphore_wait(barrier, 6)

    def go(*which):
        for one in which:
            one.start()
            used.append(one)

    def came(*which):
        for one in which:
            one.wait_recv()

    def recips(j):
        for e in range(2):
            def step(i, _):
                at_rows = pl.ds(pl.multiple_of(i * 16, 16), 16)
                rc[e, j, at_rows, :] = 1.0 / (ei[j, e, at_rows, :].astype(jnp.float32) + DAMPING)
                return 0
            lax.fori_loop(0, 8, step, 0)

    def code_of(slot):
        at_rows = pl.ds(pl.multiple_of(slot * T, T), T)
        return at_rows, acts[at_rows, 768:896].astype(jnp.float32)

    def turn_acts(slot, _):
        at_rows, code = code_of(slot)
        second = jnp.concatenate([code] * 6, axis=1) >= 4.0
        both = [
            lax.dot_general(
                acts[at_rows, 0:768], bit[e], (((1,), (1,)), ((), ())),
                preferred_element_type=jnp.float32,
            )
            for e in range(2)
        ]
        rot_a[at_rows, :] = jnp.where(second, both[1], both[0]).astype(jnp.bfloat16)
        return 0

    def columns(first, last):
        def turn_grads(slot, _):
            at_rows, code = code_of(slot)
            second = jnp.concatenate([code] * 2, axis=1) >= 4.0
            both = [
                jnp.dot(
                    rows[at_rows, :],
                    jnp.concatenate([bo[first, e], bo[last, e]], axis=1),
                    preferred_element_type=jnp.float32,
                )
                for e in range(2)
            ]
            gt[slot] = jnp.where(second, both[1], both[0]).T.astype(jnp.bfloat16)
            return 0

        def score(slot, _):
            at_rows, code = code_of(slot)
            wide = jnp.concatenate([code] * 6, axis=1)
            ra = rot_a[at_rows, :].astype(jnp.float32)
            for doc in range(DOCS_DEV):
                image = jnp.zeros((2 * T, T), jnp.float32)
                for e in range(2):
                    kept = jnp.where(wide == float(4 * e + doc), ra, 0.0).astype(jnp.bfloat16)
                    summed = jnp.dot(gt[slot], kept, preferred_element_type=jnp.float32)
                    scale = jnp.concatenate([rc[e, first], rc[e, last]], axis=0)
                    mat = (summed * scale).astype(jnp.bfloat16)
                    image = image + jnp.dot(mat, qat[e], preferred_element_type=jnp.float32)
                part = jnp.sum(image * qgt[...], axis=0, keepdims=True)
                tok[slot, doc : doc + 1, :] = tok[slot, doc : doc + 1, :] + part
            return 0

        return turn_grads, score

    def each(lo, hi, step):
        lax.fori_loop(lo, hi, step, 0)

    go(pk_z2, acts_y, *rows_y, ei_c, bo_c)
    here[0].wait()
    came(pk_z2)
    go(pk_z1, acts_z)
    for k in range(PARTS):
        go(rows_z[k], bo_z[k])
    go(ei_z)
    for one in here[1:]:
        one.wait()
    came(pk_z1)
    go(pk_y)
    turn0, score0 = columns(0, 2)
    turn1, score1 = columns(1, 3)
    recips(0)
    came(acts_z)
    go(acts_d)
    came(rows_z[0])
    go(rows_d[0])
    came(ei_c, bo_c)
    came(pk_y)
    go(pk_c1, pk_x)
    came(bo_z[0])
    go(bo_x[0])
    came(rows_z[1])
    go(rows_d[1])
    each(0, 1, turn0)
    for k in range(1, PARTS):
        came(bo_z[k])
        go(bo_x[k])
        if k < PARTS - 1:
            came(rows_z[k + 1])
            go(rows_d[k + 1])
    came(ei_z)
    go(ei_x, ei_c1, bo_c1)
    recips(2)
    each(1, 2, turn0)
    came(acts_y, *rows_y)
    each(2, 3, turn0)
    came(pk_x)
    go(pk_c2)
    came(pk_c1, pk_c2)

    for other in range(16):
        oc, oy, oz = other % 2, (other // 2) % 2, other // 4
        slot = (
            jnp.where(z // 2 != oz // 2, 1, 0)
            + jnp.where(z % 2 != oz % 2, 2, 0)
            + jnp.where(y != oy, 4, 0)
            + jnp.where(c != oc, 8, 0)
        )
        for e in range(2):
            bit[e, 48 * other : 48 * other + 48, :] = biq[e, slot, 0:48, :]
        qn[16 * other : 16 * other + 16, :] = biq[0, slot, 48:64, :]

    s_at = lax.broadcasted_iota(jnp.int32, (T, 2 * T), 0)
    r_at = lax.broadcasted_iota(jnp.int32, (T, 2 * T), 1)
    quarter = []
    for j in range(4):
        pick = jnp.where(r_at == 4 * s_at + j, 1.0, 0.0).astype(jnp.bfloat16)
        quarter.append(
            jnp.dot(pick, qn[...], preferred_element_type=jnp.float32).astype(jnp.bfloat16)
        )
    Q = 4 * T
    rows[Q : Q + T, 0:768] = quarter[0]
    rows[Q : Q + T, 768:1536] = quarter[1]
    rows[Q : Q + T, 1536:2048] = quarter[2][:, 0:512]
    acts[Q : Q + T, 0:256] = quarter[2][:, 512:768]
    acts[Q : Q + T, 256:896] = quarter[3][:, 0:640]
    ident = quarter[3][:, 640:768].astype(jnp.float32)

    each(0, 3, turn_acts)
    each(4, 5, turn_acts)
    _, qcode = code_of(4)
    qsecond = jnp.concatenate([qcode] * 6, axis=1) >= 4.0
    turned = rot_a[Q : Q + T, :].astype(jnp.float32)
    qat[0] = jnp.where(qsecond, 0.0, turned).T.astype(jnp.bfloat16)
    qat[1] = jnp.where(qsecond, turned, 0.0).T.astype(jnp.bfloat16)
    tok[...] = jnp.zeros_like(tok)

    each(4, 5, turn0)
    qgt[...] = gt[4].astype(jnp.float32)
    each(0, 3, score0)
    came(acts_d, *rows_d)
    each(3, 4, turn_acts)
    each(3, 4, turn0)
    came(ei_x, *bo_x)
    go(ei_c2, bo_c2)
    each(3, 4, score0)
    recips(1)
    came(ei_c1, bo_c1, ei_c2, bo_c2)
    recips(3)
    each(0, 5, turn1)
    qgt[...] = gt[4].astype(jnp.float32)
    each(1, 4, score1)
    go(tok_z, tok_y, tok_d)
    each(0, 1, score1)
    s_f = lax.broadcasted_iota(jnp.int32, (T, T), 0)
    q_f = lax.broadcasted_iota(jnp.int32, (T, T), 1).astype(jnp.float32)
    owner = ((s_f // 4) * QRY_DEV).astype(jnp.float32)
    table = jnp.where(owner + ident == q_f, 1.0, 0.0)
    came(tok_z, tok_y, tok_d)
    total = tok[0] + got[0] + got[1] + got[2]
    res = jnp.dot(
        total, table, precision=lax.Precision.HIGHEST, preferred_element_type=jnp.float32
    )
    out_ref[...] = res[0:4, 0:32]
    for one in used:
        one.wait_send()


def fused(
    train_acts, train_grads, train_expert, train_doc, query_acts, query_grads,
    query_expert, query_ids, basis_out, basis_in, eigenvalues,
):
    bf = jnp.bfloat16
    code = (train_expert * 4 + train_doc[:, None]).astype(bf)
    acts_in = jnp.concatenate([train_acts, jnp.broadcast_to(code, (LANES, LANES))], axis=1)
    qcode = jnp.broadcast_to((query_expert * 4).astype(bf), (4, LANES))
    qident = jnp.broadcast_to(query_ids.astype(bf)[:, None], (4, LANES))
    qpack = jnp.concatenate([query_grads, query_acts, qcode, qident], axis=1).reshape(1, 16, 768)
    qpack = jnp.concatenate([qpack, jnp.zeros_like(qpack)], axis=0)
    pk_in = jnp.concatenate([jnp.swapaxes(basis_in, 1, 2), qpack], axis=1)
    anywhere = pl.BlockSpec(memory_space=pl.ANY)
    f32 = jnp.float32
    return pl.pallas_call(
        kernel,
        out_shape=jax.ShapeDtypeStruct((4, 32), f32),
        in_specs=[anywhere] * 5,
        out_specs=pl.BlockSpec(memory_space=pltpu.VMEM),
        scratch_shapes=[
            pltpu.VMEM((5 * LANES, 2048), bf),
            pltpu.VMEM((5 * LANES, 896), bf),
            pltpu.VMEM((4, 2, 2048, LANES), bf),
            pltpu.VMEM((4, 2, LANES, 768), bf),
            pltpu.VMEM((2, 16, 64, 768), bf),
            pltpu.VMEM((2, 768, 768), bf),
            pltpu.VMEM((5 * LANES, 768), bf),
            pltpu.VMEM((2 * LANES, 768), bf),
            pltpu.VMEM((2, 768, LANES), bf),
            pltpu.VMEM((2 * LANES, LANES), f32),
            pltpu.VMEM((2, 4, LANES, 768), f32),
            pltpu.VMEM((5, 2 * LANES, LANES), bf),
            pltpu.VMEM((4, 8, LANES), f32),
            pltpu.VMEM((3, 8, LANES), f32),
            pltpu.SemaphoreType.DMA((COPIES,)),
            pltpu.SemaphoreType.DMA((COPIES,)),
            pltpu.SemaphoreType.DMA((LOCALS,)),
        ],
        compiler_params=pltpu.CompilerParams(
            collective_id=0, has_side_effects=True, vmem_limit_bytes=60 * 2**20
        ),
    )(train_grads, acts_in, basis_out, eigenvalues, pk_in)


def slot_table(experts, capacity, count):
    rows = experts.shape[0]
    place = jnp.arange(rows, dtype=jnp.int32)
    ahead = (experts[:, None] == experts[None, :]) & (place[None, :] < place[:, None])
    rank = jnp.sum(ahead.astype(jnp.int32), axis=1)
    target = experts * capacity + rank
    source = (
        jnp.zeros((count * capacity,), jnp.int32).at[target].set(jnp.arange(rows, dtype=jnp.int32))
    )
    filled = jnp.zeros((count * capacity,), jnp.int32).at[target].set(1)
    return (source.reshape(count, capacity), filled.reshape(count, capacity))


def turner(rows, piece):
    return jnp.einsum("ecd,edn->ecn", rows, piece, preferred_element_type=jnp.float32)


def body(
    train_acts,
    train_grads,
    train_expert,
    train_doc,
    query_acts,
    query_grads,
    query_expert,
    query_ids,
    basis_out,
    basis_in,
    eigenvalues,
):
    count = basis_out.shape[0]
    train_src, train_fill = slot_table(train_expert[:, 0], CAP, count)
    query_src, query_fill = slot_table(query_expert[:, 0], QCAP, count)
    source = jnp.concatenate([train_src, query_src + train_acts.shape[0]], axis=1)
    filled = jnp.concatenate([train_fill, query_fill], axis=1)
    weight = filled.astype(jnp.bfloat16)[:, :, None]
    grads_in = jnp.concatenate([train_grads, query_grads], axis=0)[source] * weight
    acts_in = jnp.concatenate([train_acts, query_acts], axis=0)[source] * weight
    slot_doc = train_doc[train_src]
    queries_total = QRY_DEV * lax.axis_size("blk")
    global_ids = jnp.where(
        query_fill == 1, lax.axis_index("blk") * QRY_DEV + query_ids[query_src], -1
    )
    rot_grads = turner(grads_in, lax.all_gather(basis_out, "blk", axis=2, tiled=True))
    rot_acts = turner(acts_in, lax.all_gather(basis_in, "blk", axis=2, tiled=True))
    rot_grads = rot_grads.astype(jnp.bfloat16)
    rot_acts = rot_acts.astype(jnp.bfloat16)
    train_g = rot_grads[:, :CAP]
    train_a = rot_acts[:, :CAP]
    query_g = rot_grads[:, CAP:]
    query_a = rot_acts[:, CAP:]
    doc_masks = [
        ((slot_doc == doc) & (train_fill == 1)).astype(jnp.bfloat16) for doc in range(DOCS_DEV)
    ]
    scale = lax.all_gather(eigenvalues, "blk", axis=1, tiled=True).astype(jnp.float32) + DAMPING
    mats = []
    for mask in doc_masks:
        summed = jnp.einsum(
            "ecn,ecf->enf", train_g * mask[:, :, None], train_a, preferred_element_type=jnp.float32
        )
        mats.append((summed / scale).astype(jnp.bfloat16))
    doc_mats = jnp.stack(mats)
    piece_g, piece_a, piece_ids = lax.all_gather(
        (query_g, query_a, global_ids), "blk", axis=1, tiled=True
    )
    image = jnp.einsum("esf,kedf->kesd", piece_a, doc_mats, preferred_element_type=jnp.float32)
    token = jnp.einsum("kesd,esd->esk", image, piece_g.astype(jnp.float32))
    table = (
        piece_ids.reshape(-1)[:, None] == jnp.arange(queries_total, dtype=jnp.int32)[None, :]
    ).astype(jnp.float32)
    return jnp.dot(token.reshape(-1, DOCS_DEV).T, table, precision=lax.Precision.HIGHEST)


def solution(mesh):
    in_specs = (
        P(("groups", "blk"), None),
        P(("groups", "blk"), None),
        P(("groups", "blk"), None),
        P(("groups", "blk")),
        P("blk", None),
        P("blk", None),
        P("blk", None),
        P("blk"),
        P(None, None, "blk"),
        P(None, None, "blk"),
        P(None, "blk", None),
    )
    out_specs = P(("groups", "blk"), None)
    sizes = (mesh.shape["groups"], mesh.shape["blk"])
    chosen = fused if sizes == (2, 16) else body
    return jax.shard_map(chosen, mesh=mesh, in_specs=in_specs, out_specs=out_specs, check_vma=False)
```

```python
import jax
import jax.numpy as jnp
from jax import lax
from jax.experimental import pallas as pl
from jax.experimental.pallas import tpu as pltpu
from jax.sharding import PartitionSpec as P

DOCS_DEV = 4
QRY_DEV = 2
CAP = 96
QCAP = 3
DAMPING = 0.05
LANES = 128
COPIES = 51
PARTS = 4
LOCALS = 5
MESH = pl.DeviceIdType.MESH


def kernel(
    grads_in, acts_in, bo_in, ei_in, pk_in, out_ref,
    rows, acts, bo, ei, biq, bit, rot_a, qn, qat, qgt, rc, gt, tok, got,
    send, recv, local,
):
    x = lax.axis_index("groups")
    b = lax.axis_index("blk")
    c, y, z = b % 2, (b // 2) % 2, b // 4
    z1 = z + 1 - 2 * (z % 2)
    z2 = (z + 2) % 4

    def at(xx, zz, yy, cc):
        return (xx, (zz * 2 + yy) * 2 + cc)

    to_z1, to_z2 = at(x, z1, y, c), at(x, z2, y, c)
    to_y, to_x = at(x, z, 1 - y, c), at(1 - x, z, y, c)
    to_c, to_d = at(x, z, y, 1 - c), at(x, z1, 1 - y, c)
    used = []
    barrier = pltpu.get_barrier_semaphore()
    for peer in (to_z1, to_z2, to_y, to_x, to_c, to_d):
        pl.semaphore_signal(barrier, inc=1, device_id=peer, device_id_type=MESH)

    def put(i, src, dst, peer):
        return pltpu.make_async_remote_copy(
            src_ref=src, dst_ref=dst, send_sem=send.at[i], recv_sem=recv.at[i],
            device_id=peer, device_id_type=MESH,
        )

    T = LANES
    ox = 1 - x
    R, K = T // PARTS, 2048 // PARTS
    count = [0]

    def next_put(src, dst, peer):
        count[0] += 1
        return put(count[0] - 1, src, dst, peer)

    def row_parts(src, first, peer):
        return [
            next_put(src.at[pl.ds(R * k, R)], rows.at[pl.ds(first + R * k, R)], peer)
            for k in range(PARTS)
        ]

    rows_z = row_parts(grads_in, T, to_z1)
    rows_y = row_parts(grads_in, 2 * T, to_y)
    rows_d = row_parts(rows.at[pl.ds(T, T)], 3 * T, to_y)
    bo_z = [
        next_put(bo_in.at[x, pl.ds(K * k, K)], bo.at[1, x, pl.ds(K * k, K)], to_z2)
        for k in range(PARTS)
    ]
    bo_x = [
        next_put(bo.at[1, x, pl.ds(K * k, K)], bo.at[1, x, pl.ds(K * k, K)], to_x)
        for k in range(PARTS)
    ]
    acts_z = next_put(acts_in, acts.at[pl.ds(T, T)], to_z1)
    acts_y = next_put(acts_in, acts.at[pl.ds(2 * T, T)], to_y)
    acts_d = next_put(acts.at[pl.ds(T, T)], acts.at[pl.ds(3 * T, T)], to_y)
    ei_z = next_put(ei_in.at[x], ei.at[1, x], to_z2)
    ei_x = next_put(ei.at[1, x], ei.at[1, x], to_x)
    bo_c = next_put(bo_in, bo.at[2], to_c)
    ei_c = next_put(ei_in, ei.at[2], to_c)
    bo_c1 = next_put(bo.at[1, x], bo.at[3, x], to_c)
    ei_c1 = next_put(ei.at[1, x], ei.at[3, x], to_c)
    bo_c2 = next_put(bo.at[1, ox], bo.at[3, ox], to_c)
    ei_c2 = next_put(ei.at[1, ox], ei.at[3, ox], to_c)
    pk_z2 = next_put(pk_in.at[x], biq.at[x, 1], to_z2)
    own = pk_in.at[x]
    pk_z1 = [next_put(own if k == 0 else biq.at[x, k], biq.at[x, 2 + k], to_z1) for k in range(2)]
    pk_y = [next_put(own if k == 0 else biq.at[x, k], biq.at[x, 4 + k], to_y) for k in range(4)]
    pk_x = [next_put(own if k == 0 else biq.at[x, k], biq.at[x, k], to_x) for k in range(8)]
    pk_c1 = next_put(biq.at[x, pl.ds(0, 8)], biq.at[x, pl.ds(8, 8)], to_c)
    pk_c2 = next_put(biq.at[ox, pl.ds(0, 8)], biq.at[ox, pl.ds(8, 8)], to_c)
    tok_z = next_put(tok.at[1], got.at[0], to_z1)
    tok_y = next_put(tok.at[2], got.at[1], to_y)
    tok_d = next_put(tok.at[3], got.at[2], to_d)
    here = [
        pltpu.make_async_copy(pk_in.at[x], biq.at[x, 0], local.at[0]),
        pltpu.make_async_copy(grads_in, rows.at[pl.ds(0, T)], local.at[1]),
        pltpu.make_async_copy(acts_in, acts.at[pl.ds(0, T)], local.at[2]),
        pltpu.make_async_copy(bo_in, bo.at[0], local.at[3]),
        pltpu.make_async_copy(ei_in, ei.at[0], local.at[4]),
    ]
    for one in here:
        one.start()
    pl.semaphore_wait(barrier, 6)

    def go(*which):
        for one in which:
            one.start()
            used.append(one)

    def came(*which):
        for one in which:
            one.wait_recv()

    def recips(j):
        for e in range(2):
            def step(i, _):
                at_rows = pl.ds(pl.multiple_of(i * 16, 16), 16)
                rc[e, j, at_rows, :] = 1.0 / (ei[j, e, at_rows, :].astype(jnp.float32) + DAMPING)
                return 0
            lax.fori_loop(0, 8, step, 0)

    def code_of(slot):
        at_rows = pl.ds(pl.multiple_of(slot * T, T), T)
        return at_rows, acts[at_rows, 768:896].astype(jnp.float32)

    def turn_acts(slot, _):
        at_rows, code = code_of(slot)
        second = jnp.concatenate([code] * 6, axis=1) >= 4.0
        both = [
            lax.dot_general(
                acts[at_rows, 0:768], bit[e], (((1,), (1,)), ((), ())),
                preferred_element_type=jnp.float32,
            )
            for e in range(2)
        ]
        rot_a[at_rows, :] = jnp.where(second, both[1], both[0]).astype(jnp.bfloat16)
        return 0

    def columns(first, last):
        def turn_grads(slot, _):
            at_rows, code = code_of(slot)
            second = jnp.concatenate([code] * 2, axis=1) >= 4.0
            both = [
                jnp.dot(
                    rows[at_rows, :],
                    jnp.concatenate([bo[first, e], bo[last, e]], axis=1),
                    preferred_element_type=jnp.float32,
                )
                for e in range(2)
            ]
            gt[slot] = jnp.where(second, both[1], both[0]).T.astype(jnp.bfloat16)
            return 0

        def score(slot, _):
            at_rows, code = code_of(slot)
            wide = jnp.concatenate([code] * 6, axis=1)
            ra = rot_a[at_rows, :].astype(jnp.float32)
            for doc in range(DOCS_DEV):
                image = jnp.zeros((2 * T, T), jnp.float32)
                for e in range(2):
                    kept = jnp.where(wide == float(4 * e + doc), ra, 0.0).astype(jnp.bfloat16)
                    summed = jnp.dot(gt[slot], kept, preferred_element_type=jnp.float32)
                    scale = jnp.concatenate([rc[e, first], rc[e, last]], axis=0)
                    mat = (summed * scale).astype(jnp.bfloat16)
                    image = image + jnp.dot(mat, qat[e], preferred_element_type=jnp.float32)
                part = jnp.sum(image * qgt[...], axis=0, keepdims=True)
                tok[slot, doc : doc + 1, :] = tok[slot, doc : doc + 1, :] + part
            return 0

        return turn_grads, score

    def each(lo, hi, step):
        lax.fori_loop(lo, hi, step, 0)

    go(pk_z2, pk_z1[0], pk_y[0], pk_x[0], rows_y[0], rows_z[0], ei_c, bo_c)
    came(pk_z2)
    go(pk_z1[1], pk_y[1], pk_x[1], rows_y[1], acts_z, bo_z[0])
    came(pk_z1[0])
    go(pk_y[2], pk_x[2], rows_y[2], rows_z[1], bo_z[1])
    came(pk_z1[1])
    go(pk_y[3], pk_x[3], rows_y[3], acts_y)
    go(rows_z[2], bo_z[2], rows_z[3], bo_z[3], ei_z)
    turn0, score0 = columns(0, 2)
    turn1, score1 = columns(1, 3)
    came(pk_y[0])
    go(pk_x[4])
    came(rows_z[0], acts_z)
    go(rows_d[0], acts_d)
    came(pk_y[1])
    go(pk_x[5])
    came(bo_z[0])
    go(bo_x[0])
    came(pk_y[2])
    go(pk_x[6])
    came(pk_y[3])
    here[0].wait()
    go(pk_x[7], pk_c1)
    came(rows_z[1])
    go(rows_d[1])
    came(bo_z[1])
    go(bo_x[1])
    for one in here[1:]:
        one.wait()
    recips(0)
    came(rows_z[2])
    go(rows_d[2])
    came(bo_z[2])
    go(bo_x[2])
    came(ei_c, bo_c)
    each(0, 1, turn0)
    recips(2)
    came(*pk_x)
    go(pk_c2)
    came(rows_z[3])
    go(rows_d[3])
    came(bo_z[3], ei_z)
    go(bo_x[3], ei_x, ei_c1, bo_c1)
    each(1, 2, turn0)
    came(acts_y, *rows_y)
    each(2, 3, turn0)
    came(pk_c1, pk_c2)

    for other in range(16):
        oc, oy, oz = other % 2, (other // 2) % 2, other // 4
        slot = (
            jnp.where(z // 2 != oz // 2, 1, 0)
            + jnp.where(z % 2 != oz % 2, 2, 0)
            + jnp.where(y != oy, 4, 0)
            + jnp.where(c != oc, 8, 0)
        )
        for e in range(2):
            bit[e, 48 * other : 48 * other + 48, :] = biq[e, slot, 0:48, :]
        qn[16 * other : 16 * other + 16, :] = biq[0, slot, 48:64, :]

    s_at = lax.broadcasted_iota(jnp.int32, (T, 2 * T), 0)
    r_at = lax.broadcasted_iota(jnp.int32, (T, 2 * T), 1)
    quarter = []
    for j in range(4):
        pick = jnp.where(r_at == 4 * s_at + j, 1.0, 0.0).astype(jnp.bfloat16)
        quarter.append(
            jnp.dot(pick, qn[...], preferred_element_type=jnp.float32).astype(jnp.bfloat16)
        )
    Q = 4 * T
    rows[Q : Q + T, 0:768] = quarter[0]
    rows[Q : Q + T, 768:1536] = quarter[1]
    rows[Q : Q + T, 1536:2048] = quarter[2][:, 0:512]
    acts[Q : Q + T, 0:256] = quarter[2][:, 512:768]
    acts[Q : Q + T, 256:896] = quarter[3][:, 0:640]
    ident = quarter[3][:, 640:768].astype(jnp.float32)

    each(0, 3, turn_acts)
    each(4, 5, turn_acts)
    _, qcode = code_of(4)
    qsecond = jnp.concatenate([qcode] * 6, axis=1) >= 4.0
    turned = rot_a[Q : Q + T, :].astype(jnp.float32)
    qat[0] = jnp.where(qsecond, 0.0, turned).T.astype(jnp.bfloat16)
    qat[1] = jnp.where(qsecond, turned, 0.0).T.astype(jnp.bfloat16)
    tok[...] = jnp.zeros_like(tok)

    each(4, 5, turn0)
    qgt[...] = gt[4].astype(jnp.float32)
    each(0, 3, score0)
    came(acts_d, *rows_d)
    each(3, 4, turn_acts)
    each(3, 4, turn0)
    came(ei_x, *bo_x)
    go(ei_c2, bo_c2)
    each(3, 4, score0)
    recips(1)
    came(ei_c1, bo_c1, ei_c2, bo_c2)
    recips(3)
    each(0, 5, turn1)
    qgt[...] = gt[4].astype(jnp.float32)
    each(1, 4, score1)
    go(tok_z, tok_y, tok_d)
    each(0, 1, score1)
    s_f = lax.broadcasted_iota(jnp.int32, (T, T), 0)
    q_f = lax.broadcasted_iota(jnp.int32, (T, T), 1).astype(jnp.float32)
    owner = ((s_f // 4) * QRY_DEV).astype(jnp.float32)
    table = jnp.where(owner + ident == q_f, 1.0, 0.0)
    came(tok_z, tok_y, tok_d)
    total = tok[0] + got[0] + got[1] + got[2]
    res = jnp.dot(
        total, table, precision=lax.Precision.HIGHEST, preferred_element_type=jnp.float32
    )
    out_ref[...] = res[0:4, 0:32]
    for one in used:
        one.wait_send()


def fused(
    train_acts, train_grads, train_expert, train_doc, query_acts, query_grads,
    query_expert, query_ids, basis_out, basis_in, eigenvalues,
):
    bf = jnp.bfloat16
    code = (train_expert * 4 + train_doc[:, None]).astype(bf)
    acts_in = jnp.concatenate([train_acts, jnp.broadcast_to(code, (LANES, LANES))], axis=1)
    qcode = jnp.broadcast_to((query_expert * 4).astype(bf), (4, LANES))
    qident = jnp.broadcast_to(query_ids.astype(bf)[:, None], (4, LANES))
    qpack = jnp.concatenate([query_grads, query_acts, qcode, qident], axis=1).reshape(1, 16, 768)
    qpack = jnp.concatenate([qpack, jnp.zeros_like(qpack)], axis=0)
    pk_in = jnp.concatenate([jnp.swapaxes(basis_in, 1, 2), qpack], axis=1)
    anywhere = pl.BlockSpec(memory_space=pl.ANY)
    f32 = jnp.float32
    return pl.pallas_call(
        kernel,
        out_shape=jax.ShapeDtypeStruct((4, 32), f32),
        in_specs=[anywhere] * 5,
        out_specs=pl.BlockSpec(memory_space=pltpu.VMEM),
        scratch_shapes=[
            pltpu.VMEM((5 * LANES, 2048), bf),
            pltpu.VMEM((5 * LANES, 896), bf),
            pltpu.VMEM((4, 2, 2048, LANES), bf),
            pltpu.VMEM((4, 2, LANES, 768), bf),
            pltpu.VMEM((2, 16, 64, 768), bf),
            pltpu.VMEM((2, 768, 768), bf),
            pltpu.VMEM((5 * LANES, 768), bf),
            pltpu.VMEM((2 * LANES, 768), bf),
            pltpu.VMEM((2, 768, LANES), bf),
            pltpu.VMEM((2 * LANES, LANES), f32),
            pltpu.VMEM((2, 4, LANES, 768), f32),
            pltpu.VMEM((5, 2 * LANES, LANES), bf),
            pltpu.VMEM((4, 8, LANES), f32),
            pltpu.VMEM((3, 8, LANES), f32),
            pltpu.SemaphoreType.DMA((COPIES,)),
            pltpu.SemaphoreType.DMA((COPIES,)),
            pltpu.SemaphoreType.DMA((LOCALS,)),
        ],
        compiler_params=pltpu.CompilerParams(
            collective_id=0, has_side_effects=True, vmem_limit_bytes=60 * 2**20
        ),
    )(train_grads, acts_in, basis_out, eigenvalues, pk_in)


def slot_table(experts, capacity, count):
    rows = experts.shape[0]
    place = jnp.arange(rows, dtype=jnp.int32)
    ahead = (experts[:, None] == experts[None, :]) & (place[None, :] < place[:, None])
    rank = jnp.sum(ahead.astype(jnp.int32), axis=1)
    target = experts * capacity + rank
    source = (
        jnp.zeros((count * capacity,), jnp.int32).at[target].set(jnp.arange(rows, dtype=jnp.int32))
    )
    filled = jnp.zeros((count * capacity,), jnp.int32).at[target].set(1)
    return (source.reshape(count, capacity), filled.reshape(count, capacity))


def turner(rows, piece):
    return jnp.einsum("ecd,edn->ecn", rows, piece, preferred_element_type=jnp.float32)


def body(
    train_acts,
    train_grads,
    train_expert,
    train_doc,
    query_acts,
    query_grads,
    query_expert,
    query_ids,
    basis_out,
    basis_in,
    eigenvalues,
):
    count = basis_out.shape[0]
    train_src, train_fill = slot_table(train_expert[:, 0], CAP, count)
    query_src, query_fill = slot_table(query_expert[:, 0], QCAP, count)
    source = jnp.concatenate([train_src, query_src + train_acts.shape[0]], axis=1)
    filled = jnp.concatenate([train_fill, query_fill], axis=1)
    weight = filled.astype(jnp.bfloat16)[:, :, None]
    grads_in = jnp.concatenate([train_grads, query_grads], axis=0)[source] * weight
    acts_in = jnp.concatenate([train_acts, query_acts], axis=0)[source] * weight
    slot_doc = train_doc[train_src]
    queries_total = QRY_DEV * lax.axis_size("blk")
    global_ids = jnp.where(
        query_fill == 1, lax.axis_index("blk") * QRY_DEV + query_ids[query_src], -1
    )
    rot_grads = turner(grads_in, lax.all_gather(basis_out, "blk", axis=2, tiled=True))
    rot_acts = turner(acts_in, lax.all_gather(basis_in, "blk", axis=2, tiled=True))
    rot_grads = rot_grads.astype(jnp.bfloat16)
    rot_acts = rot_acts.astype(jnp.bfloat16)
    train_g = rot_grads[:, :CAP]
    train_a = rot_acts[:, :CAP]
    query_g = rot_grads[:, CAP:]
    query_a = rot_acts[:, CAP:]
    doc_masks = [
        ((slot_doc == doc) & (train_fill == 1)).astype(jnp.bfloat16) for doc in range(DOCS_DEV)
    ]
    scale = lax.all_gather(eigenvalues, "blk", axis=1, tiled=True).astype(jnp.float32) + DAMPING
    mats = []
    for mask in doc_masks:
        summed = jnp.einsum(
            "ecn,ecf->enf", train_g * mask[:, :, None], train_a, preferred_element_type=jnp.float32
        )
        mats.append((summed / scale).astype(jnp.bfloat16))
    doc_mats = jnp.stack(mats)
    piece_g, piece_a, piece_ids = lax.all_gather(
        (query_g, query_a, global_ids), "blk", axis=1, tiled=True
    )
    image = jnp.einsum("esf,kedf->kesd", piece_a, doc_mats, preferred_element_type=jnp.float32)
    token = jnp.einsum("kesd,esd->esk", image, piece_g.astype(jnp.float32))
    table = (
        piece_ids.reshape(-1)[:, None] == jnp.arange(queries_total, dtype=jnp.int32)[None, :]
    ).astype(jnp.float32)
    return jnp.dot(token.reshape(-1, DOCS_DEV).T, table, precision=lax.Precision.HIGHEST)


def solution(mesh):
    in_specs = (
        P(("groups", "blk"), None),
        P(("groups", "blk"), None),
        P(("groups", "blk"), None),
        P(("groups", "blk")),
        P("blk", None),
        P("blk", None),
        P("blk", None),
        P("blk"),
        P(None, None, "blk"),
        P(None, None, "blk"),
        P(None, "blk", None),
    )
    out_specs = P(("groups", "blk"), None)
    sizes = (mesh.shape["groups"], mesh.shape["blk"])
    chosen = fused if sizes == (2, 16) else body
    return jax.shard_map(chosen, mesh=mesh, in_specs=in_specs, out_specs=out_specs, check_vma=False)
```

```python
import jax
import jax.numpy as jnp
from jax import lax
from jax.experimental import pallas as pl
from jax.experimental.pallas import tpu as pltpu
from jax.sharding import PartitionSpec as P

DOCS_DEV = 4
QRY_DEV = 2
CAP = 96
QCAP = 3
DAMPING = 0.05
LANES = 128
COPIES = 51
PARTS = 4
LOCALS = 5
MESH = pl.DeviceIdType.MESH


def kernel(
    grads_in, acts_in, bo_in, ei_in, pk_in, out_ref,
    rows, acts, bo, ei, biq, bit, rot_a, qn, qat, qgt, rc, gt, tok, got,
    send, recv, local,
):
    x = lax.axis_index("groups")
    b = lax.axis_index("blk")
    c, y, z = b % 2, (b // 2) % 2, b // 4
    z1 = z + 1 - 2 * (z % 2)
    z2 = (z + 2) % 4

    def at(xx, zz, yy, cc):
        return (xx, (zz * 2 + yy) * 2 + cc)

    to_z1, to_z2 = at(x, z1, y, c), at(x, z2, y, c)
    to_y, to_x = at(x, z, 1 - y, c), at(1 - x, z, y, c)
    to_c, to_d = at(x, z, y, 1 - c), at(x, z1, 1 - y, c)
    used = []
    barrier = pltpu.get_barrier_semaphore()
    for peer in (to_z1, to_z2, to_y, to_x, to_c, to_d):
        pl.semaphore_signal(barrier, inc=1, device_id=peer, device_id_type=MESH)

    def put(i, src, dst, peer):
        return pltpu.make_async_remote_copy(
            src_ref=src, dst_ref=dst, send_sem=send.at[i], recv_sem=recv.at[i],
            device_id=peer, device_id_type=MESH,
        )

    T = LANES
    ox = 1 - x
    R, K = T // PARTS, 2048 // PARTS
    count = [0]

    def next_put(src, dst, peer):
        count[0] += 1
        return put(count[0] - 1, src, dst, peer)

    def row_parts(src, first, peer):
        return [
            next_put(src.at[pl.ds(R * k, R)], rows.at[pl.ds(first + R * k, R)], peer)
            for k in range(PARTS)
        ]

    rows_z = row_parts(grads_in, T, to_z1)
    rows_y = row_parts(grads_in, 2 * T, to_y)
    rows_d = row_parts(rows.at[pl.ds(T, T)], 3 * T, to_y)
    bo_z = [
        next_put(bo_in.at[x, pl.ds(K * k, K)], bo.at[1, x, pl.ds(K * k, K)], to_z2)
        for k in range(PARTS)
    ]
    bo_x = [
        next_put(bo.at[1, x, pl.ds(K * k, K)], bo.at[1, x, pl.ds(K * k, K)], to_x)
        for k in range(PARTS)
    ]
    acts_z = next_put(acts_in, acts.at[pl.ds(T, T)], to_z1)
    acts_y = next_put(acts_in, acts.at[pl.ds(2 * T, T)], to_y)
    acts_d = next_put(acts.at[pl.ds(T, T)], acts.at[pl.ds(3 * T, T)], to_y)
    ei_z = next_put(ei_in.at[x], ei.at[1, x], to_z2)
    ei_x = next_put(ei.at[1, x], ei.at[1, x], to_x)
    bo_c = next_put(bo_in, bo.at[2], to_c)
    ei_c = next_put(ei_in, ei.at[2], to_c)
    bo_c1 = next_put(bo.at[1, x], bo.at[3, x], to_c)
    ei_c1 = next_put(ei.at[1, x], ei.at[3, x], to_c)
    bo_c2 = next_put(bo.at[1, ox], bo.at[3, ox], to_c)
    ei_c2 = next_put(ei.at[1, ox], ei.at[3, ox], to_c)
    pk_z2 = next_put(pk_in.at[x], biq.at[x, 1], to_z2)
    own = pk_in.at[x]
    pk_z1 = [next_put(own if k == 0 else biq.at[x, k], biq.at[x, 2 + k], to_z1) for k in range(2)]
    pk_y = [next_put(own if k == 0 else biq.at[x, k], biq.at[x, 4 + k], to_y) for k in range(4)]
    pk_x = [next_put(own if k == 0 else biq.at[x, k], biq.at[x, k], to_x) for k in range(8)]
    pk_c1 = next_put(biq.at[x, pl.ds(0, 8)], biq.at[x, pl.ds(8, 8)], to_c)
    pk_c2 = next_put(biq.at[ox, pl.ds(0, 8)], biq.at[ox, pl.ds(8, 8)], to_c)
    tok_z = next_put(tok.at[1], got.at[0], to_z1)
    tok_y = next_put(tok.at[2], got.at[1], to_y)
    tok_d = next_put(tok.at[3], got.at[2], to_d)
    here = [
        pltpu.make_async_copy(pk_in.at[x], biq.at[x, 0], local.at[0]),
        pltpu.make_async_copy(grads_in, rows.at[pl.ds(0, T)], local.at[1]),
        pltpu.make_async_copy(acts_in, acts.at[pl.ds(0, T)], local.at[2]),
        pltpu.make_async_copy(bo_in, bo.at[0], local.at[3]),
        pltpu.make_async_copy(ei_in, ei.at[0], local.at[4]),
    ]
    for one in here:
        one.start()
    pl.semaphore_wait(barrier, 6)

    def go(*which):
        for one in which:
            one.start()
            used.append(one)

    def came(*which):
        for one in which:
            one.wait_recv()

    def recips(j):
        for e in range(2):
            def step(i, _):
                at_rows = pl.ds(pl.multiple_of(i * 16, 16), 16)
                rc[e, j, at_rows, :] = 1.0 / (ei[j, e, at_rows, :].astype(jnp.float32) + DAMPING)
                return 0
            lax.fori_loop(0, 8, step, 0)

    def code_of(slot):
        at_rows = pl.ds(pl.multiple_of(slot * T, T), T)
        return at_rows, acts[at_rows, 768:896].astype(jnp.float32)

    def turn_acts(slot, _):
        at_rows, code = code_of(slot)
        second = jnp.concatenate([code] * 6, axis=1) >= 4.0
        both = [
            lax.dot_general(
                acts[at_rows, 0:768], bit[e], (((1,), (1,)), ((), ())),
                preferred_element_type=jnp.float32,
            )
            for e in range(2)
        ]
        rot_a[at_rows, :] = jnp.where(second, both[1], both[0]).astype(jnp.bfloat16)
        return 0

    def columns(first, last):
        def turn_grads(slot, _):
            at_rows, code = code_of(slot)
            second = jnp.concatenate([code] * 2, axis=1) >= 4.0
            both = [
                jnp.dot(
                    rows[at_rows, :],
                    jnp.concatenate([bo[first, e], bo[last, e]], axis=1),
                    preferred_element_type=jnp.float32,
                )
                for e in range(2)
            ]
            gt[slot] = jnp.where(second, both[1], both[0]).T.astype(jnp.bfloat16)
            return 0

        def score(slot, _):
            at_rows, code = code_of(slot)
            wide = jnp.concatenate([code] * 6, axis=1)
            ra = rot_a[at_rows, :].astype(jnp.float32)
            for doc in range(DOCS_DEV):
                image = jnp.zeros((2 * T, T), jnp.float32)
                for e in range(2):
                    kept = jnp.where(wide == float(4 * e + doc), ra, 0.0).astype(jnp.bfloat16)
                    summed = jnp.dot(gt[slot], kept, preferred_element_type=jnp.float32)
                    scale = jnp.concatenate([rc[e, first], rc[e, last]], axis=0)
                    mat = (summed * scale).astype(jnp.bfloat16)
                    image = image + jnp.dot(mat, qat[e], preferred_element_type=jnp.float32)
                part = jnp.sum(image * qgt[...], axis=0, keepdims=True)
                tok[slot, doc : doc + 1, :] = tok[slot, doc : doc + 1, :] + part
            return 0

        return turn_grads, score

    def each(lo, hi, step):
        lax.fori_loop(lo, hi, step, 0)

    go(pk_z2, pk_z1[0], pk_y[0], pk_x[0], rows_y[0], rows_z[0], ei_c, bo_c)
    came(pk_z2)
    go(pk_z1[1], pk_y[1], pk_x[1], rows_y[1], acts_z, ei_z, bo_z[0])
    came(pk_z1[0])
    go(pk_y[2], pk_x[2], rows_y[2], rows_z[1], bo_z[1])
    came(pk_z1[1])
    go(pk_y[3], pk_x[3], rows_y[3], acts_y)
    go(rows_z[2], bo_z[2], rows_z[3], bo_z[3])
    turn0, score0 = columns(0, 2)
    turn1, score1 = columns(1, 3)
    came(pk_y[0])
    go(pk_x[4])
    came(rows_z[0], acts_z)
    go(rows_d[0], acts_d)
    came(pk_y[1])
    go(pk_x[5])
    came(bo_z[0], ei_z)
    go(ei_x, bo_x[0])
    came(pk_y[2])
    go(pk_x[6])
    came(pk_y[3])
    here[0].wait()
    go(pk_x[7], pk_c1)
    came(rows_z[1])
    go(rows_d[1])
    came(bo_z[1])
    go(bo_x[1])
    for one in here[1:]:
        one.wait()
    recips(0)
    came(rows_z[2])
    go(rows_d[2])
    came(bo_z[2])
    go(bo_x[2])
    came(ei_c, bo_c)
    each(0, 1, turn0)
    recips(2)
    go(ei_c1)
    came(*pk_x)
    go(pk_c2)
    came(rows_z[3])
    go(rows_d[3])
    came(bo_z[3])
    go(bo_x[3], bo_c1)
    each(1, 2, turn0)
    came(acts_y, *rows_y)
    each(2, 3, turn0)
    came(pk_c1, pk_c2)

    for other in range(16):
        oc, oy, oz = other % 2, (other // 2) % 2, other // 4
        slot = (
            jnp.where(z // 2 != oz // 2, 1, 0)
            + jnp.where(z % 2 != oz % 2, 2, 0)
            + jnp.where(y != oy, 4, 0)
            + jnp.where(c != oc, 8, 0)
        )
        for e in range(2):
            bit[e, 48 * other : 48 * other + 48, :] = biq[e, slot, 0:48, :]
        qn[16 * other : 16 * other + 16, :] = biq[0, slot, 48:64, :]

    s_at = lax.broadcasted_iota(jnp.int32, (T, 2 * T), 0)
    r_at = lax.broadcasted_iota(jnp.int32, (T, 2 * T), 1)
    quarter = []
    for j in range(4):
        pick = jnp.where(r_at == 4 * s_at + j, 1.0, 0.0).astype(jnp.bfloat16)
        quarter.append(
            jnp.dot(pick, qn[...], preferred_element_type=jnp.float32).astype(jnp.bfloat16)
        )
    Q = 4 * T
    rows[Q : Q + T, 0:768] = quarter[0]
    rows[Q : Q + T, 768:1536] = quarter[1]
    rows[Q : Q + T, 1536:2048] = quarter[2][:, 0:512]
    acts[Q : Q + T, 0:256] = quarter[2][:, 512:768]
    acts[Q : Q + T, 256:896] = quarter[3][:, 0:640]
    ident = quarter[3][:, 640:768].astype(jnp.float32)

    each(0, 3, turn_acts)
    each(4, 5, turn_acts)
    _, qcode = code_of(4)
    qsecond = jnp.concatenate([qcode] * 6, axis=1) >= 4.0
    turned = rot_a[Q : Q + T, :].astype(jnp.float32)
    qat[0] = jnp.where(qsecond, 0.0, turned).T.astype(jnp.bfloat16)
    qat[1] = jnp.where(qsecond, turned, 0.0).T.astype(jnp.bfloat16)
    tok[...] = jnp.zeros_like(tok)

    each(4, 5, turn0)
    qgt[...] = gt[4].astype(jnp.float32)
    came(ei_x)
    go(ei_c2)
    each(0, 3, score0)
    recips(1)
    came(ei_c1, ei_c2)
    recips(3)
    came(acts_d, *rows_d)
    each(3, 4, turn_acts)
    each(3, 4, turn0)
    came(*bo_x)
    go(bo_c2)
    each(3, 4, score0)
    came(bo_c1, bo_c2)
    each(0, 5, turn1)
    qgt[...] = gt[4].astype(jnp.float32)
    each(1, 4, score1)
    go(tok_z, tok_y, tok_d)
    each(0, 1, score1)
    s_f = lax.broadcasted_iota(jnp.int32, (T, T), 0)
    q_f = lax.broadcasted_iota(jnp.int32, (T, T), 1).astype(jnp.float32)
    owner = ((s_f // 4) * QRY_DEV).astype(jnp.float32)
    table = jnp.where(owner + ident == q_f, 1.0, 0.0)
    came(tok_z, tok_y, tok_d)
    total = tok[0] + got[0] + got[1] + got[2]
    res = jnp.dot(
        total, table, precision=lax.Precision.HIGHEST, preferred_element_type=jnp.float32
    )
    out_ref[...] = res[0:4, 0:32]
    for one in used:
        one.wait_send()


def fused(
    train_acts, train_grads, train_expert, train_doc, query_acts, query_grads,
    query_expert, query_ids, basis_out, basis_in, eigenvalues,
):
    bf = jnp.bfloat16
    code = (train_expert * 4 + train_doc[:, None]).astype(bf)
    acts_in = jnp.concatenate([train_acts, jnp.broadcast_to(code, (LANES, LANES))], axis=1)
    qcode = jnp.broadcast_to((query_expert * 4).astype(bf), (4, LANES))
    qident = jnp.broadcast_to(query_ids.astype(bf)[:, None], (4, LANES))
    qpack = jnp.concatenate([query_grads, query_acts, qcode, qident], axis=1).reshape(1, 16, 768)
    qpack = jnp.concatenate([qpack, jnp.zeros_like(qpack)], axis=0)
    pk_in = jnp.concatenate([jnp.swapaxes(basis_in, 1, 2), qpack], axis=1)
    anywhere = pl.BlockSpec(memory_space=pl.ANY)
    f32 = jnp.float32
    return pl.pallas_call(
        kernel,
        out_shape=jax.ShapeDtypeStruct((4, 32), f32),
        in_specs=[anywhere] * 5,
        out_specs=pl.BlockSpec(memory_space=pltpu.VMEM),
        scratch_shapes=[
            pltpu.VMEM((5 * LANES, 2048), bf),
            pltpu.VMEM((5 * LANES, 896), bf),
            pltpu.VMEM((4, 2, 2048, LANES), bf),
            pltpu.VMEM((4, 2, LANES, 768), bf),
            pltpu.VMEM((2, 16, 64, 768), bf),
            pltpu.VMEM((2, 768, 768), bf),
            pltpu.VMEM((5 * LANES, 768), bf),
            pltpu.VMEM((2 * LANES, 768), bf),
            pltpu.VMEM((2, 768, LANES), bf),
            pltpu.VMEM((2 * LANES, LANES), f32),
            pltpu.VMEM((2, 4, LANES, 768), f32),
            pltpu.VMEM((5, 2 * LANES, LANES), bf),
            pltpu.VMEM((4, 8, LANES), f32),
            pltpu.VMEM((3, 8, LANES), f32),
            pltpu.SemaphoreType.DMA((COPIES,)),
            pltpu.SemaphoreType.DMA((COPIES,)),
            pltpu.SemaphoreType.DMA((LOCALS,)),
        ],
        compiler_params=pltpu.CompilerParams(
            collective_id=0, has_side_effects=True, vmem_limit_bytes=60 * 2**20
        ),
    )(train_grads, acts_in, basis_out, eigenvalues, pk_in)


def slot_table(experts, capacity, count):
    rows = experts.shape[0]
    place = jnp.arange(rows, dtype=jnp.int32)
    ahead = (experts[:, None] == experts[None, :]) & (place[None, :] < place[:, None])
    rank = jnp.sum(ahead.astype(jnp.int32), axis=1)
    target = experts * capacity + rank
    source = (
        jnp.zeros((count * capacity,), jnp.int32).at[target].set(jnp.arange(rows, dtype=jnp.int32))
    )
    filled = jnp.zeros((count * capacity,), jnp.int32).at[target].set(1)
    return (source.reshape(count, capacity), filled.reshape(count, capacity))


def turner(rows, piece):
    return jnp.einsum("ecd,edn->ecn", rows, piece, preferred_element_type=jnp.float32)


def body(
    train_acts,
    train_grads,
    train_expert,
    train_doc,
    query_acts,
    query_grads,
    query_expert,
    query_ids,
    basis_out,
    basis_in,
    eigenvalues,
):
    count = basis_out.shape[0]
    train_src, train_fill = slot_table(train_expert[:, 0], CAP, count)
    query_src, query_fill = slot_table(query_expert[:, 0], QCAP, count)
    source = jnp.concatenate([train_src, query_src + train_acts.shape[0]], axis=1)
    filled = jnp.concatenate([train_fill, query_fill], axis=1)
    weight = filled.astype(jnp.bfloat16)[:, :, None]
    grads_in = jnp.concatenate([train_grads, query_grads], axis=0)[source] * weight
    acts_in = jnp.concatenate([train_acts, query_acts], axis=0)[source] * weight
    slot_doc = train_doc[train_src]
    queries_total = QRY_DEV * lax.axis_size("blk")
    global_ids = jnp.where(
        query_fill == 1, lax.axis_index("blk") * QRY_DEV + query_ids[query_src], -1
    )
    rot_grads = turner(grads_in, lax.all_gather(basis_out, "blk", axis=2, tiled=True))
    rot_acts = turner(acts_in, lax.all_gather(basis_in, "blk", axis=2, tiled=True))
    rot_grads = rot_grads.astype(jnp.bfloat16)
    rot_acts = rot_acts.astype(jnp.bfloat16)
    train_g = rot_grads[:, :CAP]
    train_a = rot_acts[:, :CAP]
    query_g = rot_grads[:, CAP:]
    query_a = rot_acts[:, CAP:]
    doc_masks = [
        ((slot_doc == doc) & (train_fill == 1)).astype(jnp.bfloat16) for doc in range(DOCS_DEV)
    ]
    scale = lax.all_gather(eigenvalues, "blk", axis=1, tiled=True).astype(jnp.float32) + DAMPING
    mats = []
    for mask in doc_masks:
        summed = jnp.einsum(
            "ecn,ecf->enf", train_g * mask[:, :, None], train_a, preferred_element_type=jnp.float32
        )
        mats.append((summed / scale).astype(jnp.bfloat16))
    doc_mats = jnp.stack(mats)
    piece_g, piece_a, piece_ids = lax.all_gather(
        (query_g, query_a, global_ids), "blk", axis=1, tiled=True
    )
    image = jnp.einsum("esf,kedf->kesd", piece_a, doc_mats, preferred_element_type=jnp.float32)
    token = jnp.einsum("kesd,esd->esk", image, piece_g.astype(jnp.float32))
    table = (
        piece_ids.reshape(-1)[:, None] == jnp.arange(queries_total, dtype=jnp.int32)[None, :]
    ).astype(jnp.float32)
    return jnp.dot(token.reshape(-1, DOCS_DEV).T, table, precision=lax.Precision.HIGHEST)


def solution(mesh):
    in_specs = (
        P(("groups", "blk"), None),
        P(("groups", "blk"), None),
        P(("groups", "blk"), None),
        P(("groups", "blk")),
        P("blk", None),
        P("blk", None),
        P("blk", None),
        P("blk"),
        P(None, None, "blk"),
        P(None, None, "blk"),
        P(None, "blk", None),
    )
    out_specs = P(("groups", "blk"), None)
    sizes = (mesh.shape["groups"], mesh.shape["blk"])
    chosen = fused if sizes == (2, 16) else body
    return jax.shard_map(chosen, mesh=mesh, in_specs=in_specs, out_specs=out_specs, check_vma=False)
```
